32 devices in a mesh: mode: 4 (over x, core), batch: 4 (over z), cores: 2 (over y).
Axes of the slice: x: 2, y: 2, z: 4, core: 2. Of those that a mesh axis runs over, the one named last changes fastest.
Arguments:
- fields: bfloat16 [4, 20, 1024, 1024], P('batch', None, ('mode', 'cores')), may hold values from -6 to 6
- lift_weight: bfloat16 [20, 128], replicated, may hold values from -1.25 to 1.25
- lift_bias: float32 [128], replicated, may hold values from -3 to 3
- first_core: bfloat16 [128, 32, 32], P('batch'), may hold values from -1 to 1
- second_core: bfloat16 [128, 32, 32], P(('mode', 'cores')), may hold values from -1 to 1
- input_core: bfloat16 [128, 32, 32], P('batch'), may hold values from -0.09375 to 0.09375
- output_core: bfloat16 [128, 2, 32, 32], P('batch'), may hold values from -3 to 3
- skip_weight: bfloat16 [128, 128], replicated, may hold values from -0.5 to 0.5
- skip_bias: float32 [128], replicated, may hold values from -3 to 3
- out_weight: bfloat16 [128, 20], replicated, may hold values from -0.5 to 0.5
- out_bias: float32 [20], replicated, may hold values from -3 to 3
Outputs:
- updated: bfloat16 [4, 20, 1024, 1024], P('batch', None, ('mode', 'cores'))
The draws below stay inside these ranges and needn't reach their ends.
All inputs are finite; a program needn't handle non-finite values.
Results may differ from the reference program's by a relative error of at most 0.012.
Values may be sent and summed in bfloat16 or wider, within the bound.
A program may use at most 256 MiB of HBM per device.

```python
import math
import jax
import jax.numpy as jnp
from jax import lax

V = 20
C = 128
NX = 1024
NY = 1024
MX = 128
MY = 128
R = 32
FIELDS = 4
ROWS_DEV = 128


def levels(key, extent, split, smallest, largest):
    level, own = 1.0, jax.random.fold_in(key, 6)
    for position, parts in split:
        steps = jnp.exp(jax.random.uniform(jax.random.fold_in(own, position), (parts,), jnp.float32, smallest / len(split), largest / len(split)))
        level = level * jnp.repeat(steps, extent[position] // parts).reshape([-1 if axis == position else 1 for axis in range(len(extent))])
    return level


def scatter_about(key, dims, width, limit, shards=(), held_as=jnp.bfloat16):
    values = jax.random.normal(key, dims, jnp.float32) * width
    if len(shards) > 0:
        values = levels(key, dims, shards, -0.22, 0.18) * values
    return jnp.clip(values, min=-limit, max=limit).astype(held_as)


def setup_inputs(seed: int = 0) -> dict:
    arg_keys = jax.random.split(jax.random.key(seed), 12)
    return {
        "fields": scatter_about(arg_keys[0], (FIELDS, V, NX, NY), 1.0, 6.0, ((0, 4), (2, 8))),
        "lift_weight": scatter_about(arg_keys[1], (V, C), V ** -0.5, 1.25),
        "lift_bias": scatter_about(arg_keys[2], (C,), 0.5, 3.0, (), jnp.float32),
        "first_core": scatter_about(arg_keys[3], (MX, R, R), R ** -0.5, 1.0, ((0, 4),)),
        "second_core": scatter_about(arg_keys[4], (MY, R, R), R ** -0.5, 1.0, ((0, 8),)),
        "input_core": scatter_about(arg_keys[5], (C, R, R), (C * R) ** -0.5, 0.09375, ((0, 4),)),
        "output_core": scatter_about(arg_keys[6], (C, 2, R, R), 0.5, 3.0, ((0, 4),)),
        "skip_weight": scatter_about(arg_keys[7], (C, C), C ** -0.5, 0.5),
        "skip_bias": scatter_about(arg_keys[8], (C,), 0.5, 3.0, (), jnp.float32),
        "out_weight": scatter_about(arg_keys[9], (C, V), C ** -0.5, 0.5),
        "out_bias": scatter_about(arg_keys[10], (V,), 0.5, 3.0, (), jnp.float32),
    }


TWO_PI = 2.0 * math.pi

def wave_pair(waves, points, length):
    phase_step = waves[:, None] * points[None, :] % length
    angles = phase_step.astype(jnp.float32) * (TWO_PI / length)
    return (jnp.cos(angles), jnp.sin(angles))

def width_forward(length, wave_count):
    points = jnp.arange(length, dtype=jnp.int32)
    waves = jnp.arange(wave_count, dtype=jnp.int32)
    cosines, sine_part = wave_pair(points, waves, length)
    stacked = jnp.stack([cosines, -sine_part], axis=1) / math.sqrt(length)
    return stacked.astype(jnp.bfloat16)

def height_forward(row_index, wave_count, length):
    waves = jnp.arange(wave_count, dtype=jnp.int32) - wave_count // 2
    cosines, sine_part = wave_pair(waves, row_index, length)
    upper = jnp.stack([cosines, sine_part], axis=1)
    lower = jnp.stack([-sine_part, cosines], axis=1)
    return (jnp.stack([upper, lower], axis=0) / math.sqrt(length)).astype(jnp.bfloat16)

def height_inverse(row_index, wave_count, length):
    waves = jnp.arange(wave_count, dtype=jnp.int32) - wave_count // 2
    cosines, sine_part = wave_pair(row_index, waves, length)
    upper = jnp.stack([cosines, -sine_part], axis=1)
    lower = jnp.stack([sine_part, cosines], axis=1)
    return (jnp.stack([upper, lower], axis=0) / math.sqrt(length)).astype(jnp.bfloat16)

def width_inverse(waves, length):
    points = jnp.arange(length, dtype=jnp.int32)
    cosines, sine_part = wave_pair(waves, points, length)
    weight = jnp.where(waves == 0, 1.0, 2.0).astype(jnp.float32)[:, None]
    stacked = jnp.stack([cosines * weight, -sine_part * weight], axis=0) / math.sqrt(length)
    return stacked.astype(jnp.bfloat16)

def as_float(value):
    return value.astype(jnp.float32)

def bias_modes(lift_bias, wave_index, length):
    real_row = jnp.where(wave_index == 0, 1.0, 0.0).astype(jnp.float32)[:, None] * (math.sqrt(length) * lift_bias)[None, :]
    return jnp.stack([real_row, jnp.zeros_like(real_row)], axis=0)

def mix_modes(spectrum, mode_factor, input_core, output_core):
    projected = jnp.einsum('qkmc,cbe->qkmbe', as_float(spectrum), as_float(input_core)).astype(jnp.bfloat16)
    carried = jnp.einsum('kmab,qkmbe->qkmae', as_float(mode_factor), as_float(projected)).astype(jnp.bfloat16)
    traced = jnp.einsum('qkmae,osea->qkmso', as_float(carried), as_float(output_core))
    real_part = traced[0, :, :, 0, :] - traced[1, :, :, 1, :]
    imaginary = traced[0, :, :, 1, :] + traced[1, :, :, 0, :]
    return jnp.stack([real_part, imaginary], axis=0).astype(jnp.bfloat16)

def reference(fields, lift_weight, lift_bias, first_core, second_core, input_core, output_core, skip_weight, skip_bias, out_weight, out_bias):
    width_table = width_forward(NY, MY)
    stored = jnp.arange(NX, dtype=jnp.int32)
    row_index = (stored % ROWS_DEV * (NX // ROWS_DEV) + stored // ROWS_DEV).astype(jnp.int32)
    height_table = height_forward(row_index, MX, NX)
    height_back = height_inverse(row_index, MX, NX)
    width_back = width_inverse(jnp.arange(MY, dtype=jnp.int32), NY)
    mode_factor = jnp.einsum('kab,mbd->kmad', as_float(first_core), as_float(second_core)).astype(jnp.bfloat16)
    bias_term = bias_modes(lift_bias, jnp.arange(MY, dtype=jnp.int32), NY)

    def one_field(single):
        lifted = (jnp.einsum('vxy,vc->xyc', as_float(single), as_float(lift_weight)) + lift_bias).astype(jnp.bfloat16)
        field_modes = jnp.einsum('vxy,ypk->xpkv', as_float(single), as_float(width_table)).astype(jnp.bfloat16)
        row_modes = (jnp.einsum('xpkv,vc->xpkc', as_float(field_modes), as_float(lift_weight)) + bias_term).astype(jnp.bfloat16)
        spectrum = jnp.einsum('qkpx,xpmc->qkmc', as_float(height_table), as_float(row_modes)).astype(jnp.bfloat16)
        mixed_modes = mix_modes(spectrum, mode_factor, input_core, output_core)
        col_modes = jnp.einsum('pxqk,qkmc->xpmc', as_float(height_back), as_float(mixed_modes)).astype(jnp.bfloat16)
        spatial = jnp.einsum('xpmc,pmy->xyc', as_float(col_modes), as_float(width_back))
        skip_term = jnp.einsum('xyc,cd->xyd', as_float(lifted), as_float(skip_weight))
        active = jax.nn.gelu(spatial + skip_term + skip_bias, approximate=False).astype(jnp.bfloat16)
        result = jnp.einsum('xyc,cv->vxy', as_float(active), as_float(out_weight)) + out_bias[:, None, None]
        return result.astype(jnp.bfloat16)
    return lax.map(one_field, fields)
```

```python
import math

import jax
import jax.numpy as jnp
import ml_dtypes
import numpy as np
from jax import lax
from jax.experimental import pallas as pl
from jax.experimental.pallas import tpu as pltpu
from jax.sharding import PartitionSpec as P

NX = 1024
NY = 1024
MX = 128
MY = 128


TWO_PI = 2.0 * math.pi


def wave_pair(waves, points, length):
    phase_step = waves[:, None] * points[None, :] % length
    angles = phase_step.astype(jnp.float32) * (TWO_PI / length)
    return (jnp.cos(angles), jnp.sin(angles))


def width_forward(length, wave_count):
    points = jnp.arange(length, dtype=jnp.int32)
    waves = jnp.arange(wave_count, dtype=jnp.int32)
    cosines, sine_part = wave_pair(points, waves, length)
    stacked = jnp.stack([cosines, -sine_part], axis=1) / math.sqrt(length)
    return stacked.astype(jnp.bfloat16)


def height_forward(row_index, wave_count, length):
    waves = jnp.arange(wave_count, dtype=jnp.int32) - wave_count // 2
    cosines, sine_part = wave_pair(waves, row_index, length)
    upper = jnp.stack([cosines, sine_part], axis=1)
    lower = jnp.stack([-sine_part, cosines], axis=1)
    return (jnp.stack([upper, lower], axis=0) / math.sqrt(length)).astype(jnp.bfloat16)


def height_inverse(row_index, wave_count, length):
    waves = jnp.arange(wave_count, dtype=jnp.int32) - wave_count // 2
    cosines, sine_part = wave_pair(row_index, waves, length)
    upper = jnp.stack([cosines, -sine_part], axis=1)
    lower = jnp.stack([sine_part, cosines], axis=1)
    return (jnp.stack([upper, lower], axis=0) / math.sqrt(length)).astype(jnp.bfloat16)


def width_inverse(waves, length):
    points = jnp.arange(length, dtype=jnp.int32)
    cosines, sine_part = wave_pair(waves, points, length)
    weight = jnp.where(waves == 0, 1.0, 2.0).astype(jnp.float32)[:, None]
    stacked = jnp.stack([cosines * weight, -sine_part * weight], axis=0) / math.sqrt(length)
    return stacked.astype(jnp.bfloat16)


def bias_modes(lift_bias, wave_index, length):
    real_row = (
        jnp.where(wave_index == 0, 1.0, 0.0).astype(jnp.float32)[:, None]
        * (math.sqrt(length) * lift_bias)[None, :]
    )
    return jnp.stack([real_row, jnp.zeros_like(real_row)], axis=0)


def lift_modes(modes, lift_weight, lift_bias, wave_index):
    lifted_modes = jnp.einsum(
        "fabpmv,vc->fabpmc", modes, lift_weight, preferred_element_type=jnp.float32
    )
    return (lifted_modes + bias_modes(lift_bias, wave_index, NY)).astype(jnp.bfloat16)


def grid_rows(stored, row_count, holder_count):
    return stored % row_count * holder_count + stored // row_count


def shards(
    fields,
    lift_weight,
    lift_bias,
    first_core,
    second_core,
    input_core,
    output_core,
    skip_weight,
    skip_bias,
    out_weight,
    out_bias,
):
    mode_count = lax.axis_size("mode")
    core_count = lax.axis_size("cores")
    row_count = fields.shape[2]
    block_size = second_core.shape[0]
    block_start = (lax.axis_index("mode") * core_count + lax.axis_index("cores")) * block_size
    local_waves = block_start + jnp.arange(block_size, dtype=jnp.int32)
    lifted = (
        jnp.einsum("fvxy,vc->fxyc", fields, lift_weight, preferred_element_type=jnp.float32)
        + lift_bias
    ).astype(jnp.bfloat16)
    field_modes = jnp.einsum(
        "fvxy,ypk->fxpkv", fields, width_forward(NY, MY), preferred_element_type=jnp.float32
    ).astype(jnp.bfloat16)
    field_modes = field_modes[:, None]
    gathered = (
        lax.all_gather(first_core, "batch", axis=0, tiled=True),
        lax.all_gather(input_core, "batch", axis=0, tiled=True),
        lax.all_gather(output_core, "batch", axis=0, tiled=True),
    )
    first_whole, input_whole, output_whole = gathered
    mode_factor = jnp.einsum(
        "kab,mbd->kmad", first_whole, second_core, preferred_element_type=jnp.float32
    ).astype(jnp.bfloat16)
    arrived = lax.all_to_all(
        field_modes, ("mode", "cores"), split_axis=4, concat_axis=2, tiled=True
    )
    rows_held = jnp.arange(NX, dtype=jnp.int32)[None, :]
    by_mode = lift_modes(arrived, lift_weight, lift_bias, local_waves)
    lead_rows = rows_held.shape[0]
    side_rows = rows_held.shape[1]
    flat_rows = grid_rows(rows_held.reshape(-1), row_count, mode_count * core_count)
    height_table = height_forward(flat_rows, MX, NX).reshape(2, MX, 2, lead_rows, side_rows)
    spectrum = jnp.einsum(
        "qkpab,fabpmc->fqkmc", height_table, by_mode, preferred_element_type=jnp.float32
    ).astype(jnp.bfloat16)
    projected = jnp.einsum(
        "fqkmc,cbe->fqkmbe", spectrum, input_whole, preferred_element_type=jnp.float32
    ).astype(jnp.bfloat16)
    carried = jnp.einsum(
        "kmab,fqkmbe->fqkmae", mode_factor, projected, preferred_element_type=jnp.float32
    ).astype(jnp.bfloat16)
    traced = jnp.einsum(
        "fqkmae,osea->fqkmso", carried, output_whole, preferred_element_type=jnp.float32
    )
    real_part = traced[:, 0, :, :, 0, :] - traced[:, 1, :, :, 1, :]
    imaginary = traced[:, 0, :, :, 1, :] + traced[:, 1, :, :, 0, :]
    mixed_modes = jnp.stack([real_part, imaginary], axis=1).astype(jnp.bfloat16)
    height_back = height_inverse(flat_rows, MX, NX).reshape(2, lead_rows, side_rows, 2, MX)
    col_modes = jnp.einsum(
        "pabqk,fqkmc->fabpmc", height_back, mixed_modes, preferred_element_type=jnp.float32
    ).astype(jnp.bfloat16)
    returned = lax.all_to_all(col_modes, ("mode", "cores"), split_axis=2, concat_axis=4, tiled=True)
    waves_held = jnp.arange(MY, dtype=jnp.int32)
    width_back = width_inverse(waves_held, NY)
    spatial = jnp.einsum(
        "fxpmc,pmy->fxyc", returned[:, 0], width_back, preferred_element_type=jnp.float32
    )
    skip_term = jnp.einsum("fxyc,cd->fxyd", lifted, skip_weight, preferred_element_type=jnp.float32)
    active = jax.nn.gelu(spatial + skip_term + skip_bias, approximate=False).astype(jnp.bfloat16)
    result = (
        jnp.einsum("fxyc,cv->fvxy", active, out_weight, preferred_element_type=jnp.float32)
        + out_bias[:, None, None]
    )
    return result.astype(jnp.bfloat16)


def cyclic_rows(row_count, holders):
    return (np.arange(row_count)[None, :] * holders + np.arange(holders)[:, None]).reshape(-1)


def host_pair(waves, points, length):
    steps = np.asarray(waves)[:, None] * np.asarray(points)[None, :] % length
    angles = steps.astype(np.float32) * np.float32(TWO_PI / length)
    return np.cos(angles), np.sin(angles)


def dense(a, b, contract=((1,), (0,))):
    return lax.dot_general(a, b, (contract, ((), ())), preferred_element_type=jnp.float32)


GROUP = 4
PACK = 16


def mix_kernel(
    arrived, height, lift, row_sum, bias_row, joined, first, back, spread,
    mixed, stacked, spectrum, blocks, closing, weights, parts, carried,
):
    group = pl.program_id(0)
    holders, lead, _ = arrived.shape
    waves = lead // 2
    rank = first.shape[1]
    variables = stacked.shape[0] // waves
    row_count = arrived.shape[2] // variables
    kx_count = mixed.shape[0] // 2
    channels = joined.shape[1]
    packs = kx_count // PACK
    groups = waves // GROUP
    span = rank * PACK
    wide = GROUP * rank

    @pl.when(group == 0)
    def _():
        for d in range(holders):
            for p in range(2):
                for v in range(variables):
                    stacked[v * waves:(v + 1) * waves, (d * 2 + p) * row_count:(d * 2 + p + 1) * row_count] = (
                        arrived[d, p * waves:(p + 1) * waves, v * row_count:(v + 1) * row_count]
                    )
        by_variable = dense(height[...], stacked[...], ((1,), (1,))).astype(jnp.bfloat16)
        for g in range(groups):
            lanes = slice(g * GROUP * channels, (g + 1) * GROUP * channels)
            spectrum[g] = (
                dense(by_variable, lift[:, lanes]) + row_sum[...] * bias_row[:, lanes]
            ).astype(jnp.bfloat16)
        down = lax.broadcasted_iota(jnp.int32, (span, span), 0) % PACK
        across = lax.broadcasted_iota(jnp.int32, (span, span), 1) % PACK
        same = down == across
        for k in range(packs):
            full = dense(first[k * span:(k + 1) * span, :], spread[...])
            blocks[k] = jnp.where(same, full, 0.0).astype(jnp.bfloat16)
        closing[...] = jnp.zeros_like(closing)
        outs = back.shape[1]
        for a in range(rank):
            for m in range(GROUP):
                closing[(a * GROUP + m) * rank:(a * GROUP + m + 1) * rank, m * outs:(m + 1) * outs] = (
                    back[a * rank:(a + 1) * rank, :]
                )

    own = spectrum[group]
    owner = lax.broadcasted_iota(jnp.int32, (channels, wide), 1) // rank
    for part in range(rank // 8):
        for b in range(8):
            block = joined[part * 8 + b]
            for m in range(GROUP):
                weights[m * channels:(m + 1) * channels, b * wide:(b + 1) * wide] = jnp.where(
                    owner == m, block, jnp.zeros_like(block)
                )
        got = dense(own, weights[...]).astype(jnp.bfloat16)
        for b in range(8):
            for q in range(2):
                parts[part * 8 + b, :, q * wide:(q + 1) * wide] = got[
                    q * kx_count:(q + 1) * kx_count, b * wide:(b + 1) * wide
                ]
    for k in range(packs):
        rows = parts[:, k * PACK:(k + 1) * PACK, :].reshape(span, 2 * wide)
        got = dense(blocks[k], rows).astype(jnp.bfloat16)
        for a in range(rank):
            for q in range(2):
                carried[q * kx_count + k * PACK:q * kx_count + (k + 1) * PACK, a * wide:(a + 1) * wide] = got[
                    a * PACK:(a + 1) * PACK, q * wide:(q + 1) * wide
                ]
    traced = dense(carried[...], closing[...])
    outs = back.shape[1]
    for m in range(GROUP):
        one = traced[:, m * outs:(m + 1) * outs]
        real = one[:kx_count, :channels] - one[kx_count:, channels:]
        imaginary = one[:kx_count, channels:] + one[kx_count:, :channels]
        mixed[:kx_count, m * channels:(m + 1) * channels] = real.astype(jnp.bfloat16)
        mixed[kx_count:, m * channels:(m + 1) * channels] = imaginary.astype(jnp.bfloat16)


def mix(arrived, height, lift, row_sum, bias_row, joined, first, back, spread):
    holders, lead, flat = arrived.shape
    waves = lead // 2
    variables = lift.shape[0] // waves
    rank, channels, _ = joined.shape
    kx2 = height.shape[0]
    kx_count = kx2 // 2
    groups = waves // GROUP
    span = rank * PACK
    wide = GROUP * rank

    def whole(a):
        return pl.BlockSpec(a.shape, lambda g: (0,) * a.ndim)

    return pl.pallas_call(
        mix_kernel,
        grid=(groups,),
        in_specs=[
            whole(arrived), whole(height), whole(lift), whole(row_sum), whole(bias_row),
            pl.BlockSpec((rank, channels, wide), lambda g: (0, 0, g)),
            whole(first), whole(back), whole(spread),
        ],
        out_specs=pl.BlockSpec((kx2, GROUP * channels), lambda g: (0, g)),
        out_shape=jax.ShapeDtypeStruct((kx2, waves * channels), jnp.bfloat16),
        scratch_shapes=[
            pltpu.VMEM((variables * waves, height.shape[1]), jnp.bfloat16),
            pltpu.VMEM((groups, kx2, GROUP * channels), jnp.bfloat16),
            pltpu.VMEM((kx_count // PACK, span, span), jnp.bfloat16),
            pltpu.VMEM((rank * wide, GROUP * back.shape[1]), jnp.bfloat16),
            pltpu.VMEM((GROUP * channels, 8 * wide), jnp.bfloat16),
            pltpu.VMEM((rank, kx_count, 2 * wide), jnp.bfloat16),
            pltpu.VMEM((kx2, rank * wide), jnp.bfloat16),
        ],
        compiler_params=pltpu.CompilerParams(vmem_limit_bytes=48 * 2**20),
        name="mix",
    )(arrived, height, lift, row_sum, bias_row, joined, first, back, spread)


def rows_kernel(table, gathered, cols, turned):
    row_count, waves, channels = turned.shape
    for p in range(2):
        got = dense(table[p * row_count:(p + 1) * row_count, :], gathered[0])
        for m in range(waves):
            turned[:, m, :] = got[:, m * channels:(m + 1) * channels]
        cols[:, p] = turned[...].astype(jnp.bfloat16)


def rows_back(table, gathered, waves):
    holders, kx2, flat = gathered.shape
    row_count = table.shape[0] // 2
    channels = flat // waves
    return pl.pallas_call(
        rows_kernel,
        grid=(holders,),
        in_specs=[
            pl.BlockSpec(table.shape, lambda d: (0, 0)),
            pl.BlockSpec((1, kx2, flat), lambda d: (d, 0, 0)),
        ],
        out_specs=pl.BlockSpec((row_count, 2, waves, channels), lambda d: (0, 0, d, 0)),
        out_shape=jax.ShapeDtypeStruct((row_count, 2, holders * waves, channels), jnp.bfloat16),
        scratch_shapes=[pltpu.VMEM((row_count, waves, channels), jnp.float32)],
        compiler_params=pltpu.CompilerParams(vmem_limit_bytes=48 * 2**20),
        name="rows_back",
    )(table, gathered)


LANES = 256


def gelu(h):
    return h * (0.5 + 0.5 * lax.erf(h * (1.0 / math.sqrt(2.0))))


def finish_kernel(fields, cols, width, skip, bias, closing, out_bias, result, turned, active):
    variables, rows, points = fields.shape
    channels = cols.shape[2]
    for x in range(rows):
        turned[x * channels:(x + 1) * channels, :] = cols[x].T

    def step(i, carry):
        start = pl.multiple_of(i * LANES, LANES)
        lanes = pl.ds(start, LANES)
        source = fields[:, :, lanes].reshape(variables * rows, LANES)
        table = width[:, lanes]
        depth = 2 * channels
        for x in range(rows // 2):
            here = slice(x * depth, (x + 1) * depth)
            total = dense(turned[here, :], table) + dense(skip[here, :], source) + bias[here, :]
            active[here, :] = gelu(total).astype(jnp.bfloat16)
        got = dense(closing[...], active[...]) + out_bias[...]
        result[:, :, lanes] = got.astype(jnp.bfloat16).reshape(variables, rows, LANES)
        return carry

    lax.fori_loop(0, points // LANES, step, 0)


def finish(fields, cols, width, skip, bias, closing, out_bias):
    variables, row_count, points = fields.shape
    depth, channels = cols.shape[1:]

    def whole(a):
        return pl.BlockSpec(a.shape, lambda i: (0,) * a.ndim)

    return pl.pallas_call(
        finish_kernel,
        grid=(row_count // PACK,),
        in_specs=[
            pl.BlockSpec((variables, PACK, points), lambda i: (0, i, 0)),
            pl.BlockSpec((PACK, depth, channels), lambda i: (i, 0, 0)),
            whole(width), whole(skip), whole(bias), whole(closing), whole(out_bias),
        ],
        out_specs=pl.BlockSpec((variables, PACK, points), lambda i: (0, i, 0)),
        out_shape=jax.ShapeDtypeStruct(fields.shape, jnp.bfloat16),
        scratch_shapes=[
            pltpu.VMEM((PACK * channels, depth), jnp.bfloat16),
            pltpu.VMEM((PACK * channels, LANES), jnp.bfloat16),
        ],
        compiler_params=pltpu.CompilerParams(vmem_limit_bytes=48 * 2**20),
        name="finish",
    )(fields, cols, width, skip, bias, closing, out_bias)


def gather_factors(first_core, input_core, output_core):
    count, rank, _ = first_core.shape
    flat = jnp.concatenate(
        [first_core.reshape(-1), input_core.reshape(-1), output_core.reshape(-1)]
    ).reshape(-1, 128)
    whole = lax.all_gather(flat, "batch", axis=0, tiled=False)
    parts = whole.shape[0]
    size = first_core.size
    whole = whole.reshape(parts, -1)
    first = whole[:, :size].reshape(parts * count, rank, rank)
    inner = whole[:, size:2 * size].reshape(parts * count, rank, rank)
    outer = whole[:, 2 * size:].reshape(parts * count, 2, rank, rank)
    return first, inner, outer


def fast_shards(
    fields, lift_weight, lift_bias, first_core, second_core, input_core, output_core,
    skip_weight, skip_bias, out_weight, out_bias,
):
    holders = lax.axis_size("mode") * lax.axis_size("cores")
    waves, rank, _ = second_core.shape
    _, variables, row_count, points = fields.shape
    channels = lift_weight.shape[1]
    fields = fields[0]
    me = lax.axis_index("mode") * lax.axis_size("cores") + lax.axis_index("cores")

    cosines, sines = host_pair(np.arange(MY), np.arange(points), points)
    root = math.sqrt(points)
    forward = np.stack([cosines, -sines], 0).reshape(2, holders, waves, points).transpose(1, 0, 2, 3)
    forward = jnp.asarray((forward.reshape(2 * MY, points) / root).astype(np.float32)).astype(jnp.bfloat16)
    weight = np.where(np.arange(MY) == 0, 1.0, 2.0).astype(np.float32)[:, None]
    width = np.concatenate([cosines * weight, -sines * weight], 0) / root
    width = jnp.asarray(width.astype(ml_dtypes.bfloat16))
    order = cyclic_rows(row_count, holders)
    root = math.sqrt(NX)
    cosines, sines = host_pair(np.arange(MX) - MX // 2, order, NX)
    cosines, sines = [t.reshape(MX, holders, row_count) / root for t in (cosines, sines)]
    upper = np.stack([cosines, sines], 2)
    lower = np.stack([-sines, cosines], 2)
    height = np.stack([upper, lower], 0).reshape(2 * MX, -1).astype(ml_dtypes.bfloat16)
    real_part = np.asarray(height, np.float32).reshape(2 * MX, holders, 2, row_count)[:, :, 0]
    row_sum = real_part.sum((1, 2), dtype=np.float64).astype(np.float32)[:, None]
    cos_t, sin_t = [t.transpose(1, 2, 0) for t in (cosines, sines)]
    up = np.concatenate([cos_t, -sin_t], 2)
    low = np.concatenate([sin_t, cos_t], 2)
    back_rows = jnp.asarray(np.concatenate([up, low], 1).astype(ml_dtypes.bfloat16))
    back_rows = lax.dynamic_index_in_dim(back_rows, me, 0, keepdims=False)

    first, inner, outer = gather_factors(first_core, input_core, output_core)
    modes = jnp.einsum(
        "ry,vxy->rvx", forward, fields, preferred_element_type=jnp.float32
    ).astype(jnp.bfloat16)
    modes = modes.reshape(holders, 2 * waves, variables * row_count)
    arrived = lax.all_to_all(modes, ("mode", "cores"), split_axis=0, concat_axis=0, tiled=True)

    same = jnp.eye(waves, dtype=jnp.bfloat16)
    lift = (lift_weight[:, None, None, :] * same[None, :, :, None]).reshape(
        variables * waves, waves * channels
    )
    is_zero = (me * waves + jnp.arange(waves) == 0).astype(jnp.float32)
    bias_value = (math.sqrt(points) * lift_bias).astype(jnp.bfloat16).astype(jnp.float32)
    bias_row = (is_zero[:, None] * bias_value[None, :]).reshape(1, -1)
    joined = jnp.einsum(
        "mbd,cde->bcme", second_core, inner, preferred_element_type=jnp.float32
    ).astype(jnp.bfloat16).reshape(rank, channels, waves * rank)
    packed = first.reshape(MX // PACK, PACK, rank, rank).transpose(0, 2, 1, 3).reshape(-1, rank)
    back = outer.transpose(3, 2, 1, 0).reshape(rank * rank, -1)
    spread = jnp.asarray(np.repeat(np.eye(rank), PACK, axis=1).astype(ml_dtypes.bfloat16))
    mixed = mix(
        arrived, jnp.asarray(height), lift, jnp.asarray(row_sum), bias_row, joined, packed, back, spread
    )
    gathered = lax.all_gather(mixed, ("mode", "cores"), axis=0, tiled=False)
    cols = rows_back(back_rows, gathered, waves).reshape(row_count, 2 * MY, channels)

    skip_wide = skip_weight.astype(jnp.float32)
    direct = jnp.dot(lift_weight.astype(jnp.float32), skip_wide, precision="highest")
    total_bias = jnp.dot(lift_bias, skip_wide, precision="highest") + skip_bias
    rows_eye = jnp.eye(PACK, dtype=jnp.float32)
    skip = (rows_eye[:, None, None, :] * direct.T[None, :, :, None]).astype(jnp.bfloat16)
    skip = skip.reshape(PACK * channels, variables * PACK)
    closing = out_weight.T[:, None, None, :] * rows_eye.astype(jnp.bfloat16)[None, :, :, None]
    closing = closing.reshape(variables * PACK, PACK * channels)
    bias = jnp.tile(total_bias, PACK)[:, None]
    last_bias = jnp.repeat(out_bias, PACK)[:, None]
    return finish(fields, cols, width, skip, bias, closing, last_bias)[None]


def solution(mesh):
    placed = (
        P("batch", None, ("mode", "cores"), None),
        P(),
        P(),
        P("batch", None, None),
        P(("mode", "cores"), None, None),
        P("batch", None, None),
        P("batch", None, None, None),
        P(),
        P(),
        P(),
        P(),
    )
    holders = mesh.shape["mode"] * mesh.shape["cores"]
    fits = MY // holders % PACK == 0 and NX // holders % 128 == 0
    return jax.shard_map(
        fast_shards if fits else shards,
        mesh=mesh,
        in_specs=placed,
        out_specs=P("batch", None, ("mode", "cores"), None),
        check_vma=False,
    )
```

```python
import functools
import math

import jax
import jax.numpy as jnp
import ml_dtypes
import numpy as np
from jax import lax
from jax.experimental import pallas as pl
from jax.experimental.pallas import tpu as pltpu
from jax.sharding import PartitionSpec as P

NX = 1024
NY = 1024
MX = 128
MY = 128


TWO_PI = 2.0 * math.pi


def wave_pair(waves, points, length):
    phase_step = waves[:, None] * points[None, :] % length
    angles = phase_step.astype(jnp.float32) * (TWO_PI / length)
    return (jnp.cos(angles), jnp.sin(angles))


def width_forward(length, wave_count):
    points = jnp.arange(length, dtype=jnp.int32)
    waves = jnp.arange(wave_count, dtype=jnp.int32)
    cosines, sine_part = wave_pair(points, waves, length)
    stacked = jnp.stack([cosines, -sine_part], axis=1) / math.sqrt(length)
    return stacked.astype(jnp.bfloat16)


def height_forward(row_index, wave_count, length):
    waves = jnp.arange(wave_count, dtype=jnp.int32) - wave_count // 2
    cosines, sine_part = wave_pair(waves, row_index, length)
    upper = jnp.stack([cosines, sine_part], axis=1)
    lower = jnp.stack([-sine_part, cosines], axis=1)
    return (jnp.stack([upper, lower], axis=0) / math.sqrt(length)).astype(jnp.bfloat16)


def height_inverse(row_index, wave_count, length):
    waves = jnp.arange(wave_count, dtype=jnp.int32) - wave_count // 2
    cosines, sine_part = wave_pair(row_index, waves, length)
    upper = jnp.stack([cosines, -sine_part], axis=1)
    lower = jnp.stack([sine_part, cosines], axis=1)
    return (jnp.stack([upper, lower], axis=0) / math.sqrt(length)).astype(jnp.bfloat16)


def width_inverse(waves, length):
    points = jnp.arange(length, dtype=jnp.int32)
    cosines, sine_part = wave_pair(waves, points, length)
    weight = jnp.where(waves == 0, 1.0, 2.0).astype(jnp.float32)[:, None]
    stacked = jnp.stack([cosines * weight, -sine_part * weight], axis=0) / math.sqrt(length)
    return stacked.astype(jnp.bfloat16)


def bias_modes(lift_bias, wave_index, length):
    real_row = (
        jnp.where(wave_index == 0, 1.0, 0.0).astype(jnp.float32)[:, None]
        * (math.sqrt(length) * lift_bias)[None, :]
    )
    return jnp.stack([real_row, jnp.zeros_like(real_row)], axis=0)


def lift_modes(modes, lift_weight, lift_bias, wave_index):
    lifted_modes = jnp.einsum(
        "fabpmv,vc->fabpmc", modes, lift_weight, preferred_element_type=jnp.float32
    )
    return (lifted_modes + bias_modes(lift_bias, wave_index, NY)).astype(jnp.bfloat16)


def grid_rows(stored, row_count, holder_count):
    return stored % row_count * holder_count + stored // row_count


def shards(
    fields,
    lift_weight,
    lift_bias,
    first_core,
    second_core,
    input_core,
    output_core,
    skip_weight,
    skip_bias,
    out_weight,
    out_bias,
):
    mode_count = lax.axis_size("mode")
    core_count = lax.axis_size("cores")
    row_count = fields.shape[2]
    block_size = second_core.shape[0]
    block_start = (lax.axis_index("mode") * core_count + lax.axis_index("cores")) * block_size
    local_waves = block_start + jnp.arange(block_size, dtype=jnp.int32)
    lifted = (
        jnp.einsum("fvxy,vc->fxyc", fields, lift_weight, preferred_element_type=jnp.float32)
        + lift_bias
    ).astype(jnp.bfloat16)
    field_modes = jnp.einsum(
        "fvxy,ypk->fxpkv", fields, width_forward(NY, MY), preferred_element_type=jnp.float32
    ).astype(jnp.bfloat16)
    field_modes = field_modes[:, None]
    gathered = (
        lax.all_gather(first_core, "batch", axis=0, tiled=True),
        lax.all_gather(input_core, "batch", axis=0, tiled=True),
        lax.all_gather(output_core, "batch", axis=0, tiled=True),
    )
    first_whole, input_whole, output_whole = gathered
    mode_factor = jnp.einsum(
        "kab,mbd->kmad", first_whole, second_core, preferred_element_type=jnp.float32
    ).astype(jnp.bfloat16)
    arrived = lax.all_to_all(
        field_modes, ("mode", "cores"), split_axis=4, concat_axis=2, tiled=True
    )
    rows_held = jnp.arange(NX, dtype=jnp.int32)[None, :]
    by_mode = lift_modes(arrived, lift_weight, lift_bias, local_waves)
    lead_rows = rows_held.shape[0]
    side_rows = rows_held.shape[1]
    flat_rows = grid_rows(rows_held.reshape(-1), row_count, mode_count * core_count)
    height_table = height_forward(flat_rows, MX, NX).reshape(2, MX, 2, lead_rows, side_rows)
    spectrum = jnp.einsum(
        "qkpab,fabpmc->fqkmc", height_table, by_mode, preferred_element_type=jnp.float32
    ).astype(jnp.bfloat16)
    projected = jnp.einsum(
        "fqkmc,cbe->fqkmbe", spectrum, input_whole, preferred_element_type=jnp.float32
    ).astype(jnp.bfloat16)
    carried = jnp.einsum(
        "kmab,fqkmbe->fqkmae", mode_factor, projected, preferred_element_type=jnp.float32
    ).astype(jnp.bfloat16)
    traced = jnp.einsum(
        "fqkmae,osea->fqkmso", carried, output_whole, preferred_element_type=jnp.float32
    )
    real_part = traced[:, 0, :, :, 0, :] - traced[:, 1, :, :, 1, :]
    imaginary = traced[:, 0, :, :, 1, :] + traced[:, 1, :, :, 0, :]
    mixed_modes = jnp.stack([real_part, imaginary], axis=1).astype(jnp.bfloat16)
    height_back = height_inverse(flat_rows, MX, NX).reshape(2, lead_rows, side_rows, 2, MX)
    col_modes = jnp.einsum(
        "pabqk,fqkmc->fabpmc", height_back, mixed_modes, preferred_element_type=jnp.float32
    ).astype(jnp.bfloat16)
    returned = lax.all_to_all(col_modes, ("mode", "cores"), split_axis=2, concat_axis=4, tiled=True)
    waves_held = jnp.arange(MY, dtype=jnp.int32)
    width_back = width_inverse(waves_held, NY)
    spatial = jnp.einsum(
        "fxpmc,pmy->fxyc", returned[:, 0], width_back, preferred_element_type=jnp.float32
    )
    skip_term = jnp.einsum("fxyc,cd->fxyd", lifted, skip_weight, preferred_element_type=jnp.float32)
    active = jax.nn.gelu(spatial + skip_term + skip_bias, approximate=False).astype(jnp.bfloat16)
    result = (
        jnp.einsum("fxyc,cv->fvxy", active, out_weight, preferred_element_type=jnp.float32)
        + out_bias[:, None, None]
    )
    return result.astype(jnp.bfloat16)


def cyclic_rows(row_count, holders):
    return (np.arange(row_count)[None, :] * holders + np.arange(holders)[:, None]).reshape(-1)


def host_pair(waves, points, length):
    steps = np.asarray(waves)[:, None] * np.asarray(points)[None, :] % length
    angles = steps.astype(np.float32) * np.float32(TWO_PI / length)
    return np.cos(angles), np.sin(angles)


def dense(a, b, contract=((1,), (0,))):
    return lax.dot_general(a, b, (contract, ((), ())), preferred_element_type=jnp.float32)


GROUP = 4
PACK = 16


def mix_kernel(
    base, arrived, height, lift, row_sum, bias_row, joined, first, back, spread,
    mixed, stacked, spectrum, blocks, closing, weights, parts, carried,
):
    group = pl.program_id(0)
    holders, lead, _ = arrived.shape
    waves = lead // 2
    rank = first.shape[1]
    variables = stacked.shape[0] // waves
    row_count = arrived.shape[2] // variables
    kx_count = mixed.shape[0] // 2
    channels = joined.shape[1]
    packs = kx_count // PACK
    groups = spectrum.shape[0]
    span = rank * PACK
    wide = GROUP * rank

    @pl.when(group == 0)
    def _():
        for d in range(holders):
            for p in range(2):
                for v in range(variables):
                    stacked[v * waves:(v + 1) * waves, (d * 2 + p) * row_count:(d * 2 + p + 1) * row_count] = (
                        arrived[d, p * waves:(p + 1) * waves, v * row_count:(v + 1) * row_count]
                    )
        by_variable = dense(height[...], stacked[...], ((1,), (1,))).astype(jnp.bfloat16)
        for g in range(groups):
            lanes = slice((base + g) * GROUP * channels, (base + g + 1) * GROUP * channels)
            spectrum[g] = (
                dense(by_variable, lift[:, lanes]) + row_sum[...] * bias_row[:, lanes]
            ).astype(jnp.bfloat16)
        down = lax.broadcasted_iota(jnp.int32, (span, span), 0) % PACK
        across = lax.broadcasted_iota(jnp.int32, (span, span), 1) % PACK
        same = down == across
        for k in range(packs):
            full = dense(first[k * span:(k + 1) * span, :], spread[...])
            blocks[k] = jnp.where(same, full, 0.0).astype(jnp.bfloat16)
        closing[...] = jnp.zeros_like(closing)
        outs = back.shape[1]
        for a in range(rank):
            for m in range(GROUP):
                closing[(a * GROUP + m) * rank:(a * GROUP + m + 1) * rank, m * outs:(m + 1) * outs] = (
                    back[a * rank:(a + 1) * rank, :]
                )

    own = spectrum[group]
    owner = lax.broadcasted_iota(jnp.int32, (channels, wide), 1) // rank
    for part in range(rank // 8):
        for b in range(8):
            block = joined[part * 8 + b]
            for m in range(GROUP):
                weights[m * channels:(m + 1) * channels, b * wide:(b + 1) * wide] = jnp.where(
                    owner == m, block, jnp.zeros_like(block)
                )
        got = dense(own, weights[...]).astype(jnp.bfloat16)
        for b in range(8):
            for q in range(2):
                parts[part * 8 + b, :, q * wide:(q + 1) * wide] = got[
                    q * kx_count:(q + 1) * kx_count, b * wide:(b + 1) * wide
                ]
    for k in range(packs):
        rows = parts[:, k * PACK:(k + 1) * PACK, :].reshape(span, 2 * wide)
        got = dense(blocks[k], rows).astype(jnp.bfloat16)
        for a in range(rank):
            for q in range(2):
                carried[q * kx_count + k * PACK:q * kx_count + (k + 1) * PACK, a * wide:(a + 1) * wide] = got[
                    a * PACK:(a + 1) * PACK, q * wide:(q + 1) * wide
                ]
    traced = dense(carried[...], closing[...])
    outs = back.shape[1]
    for m in range(GROUP):
        one = traced[:, m * outs:(m + 1) * outs]
        real = one[:kx_count, :channels] - one[kx_count:, channels:]
        imaginary = one[:kx_count, channels:] + one[kx_count:, :channels]
        mixed[:kx_count, m * channels:(m + 1) * channels] = real.astype(jnp.bfloat16)
        mixed[kx_count:, m * channels:(m + 1) * channels] = imaginary.astype(jnp.bfloat16)


def mix(base, groups, arrived, height, lift, row_sum, bias_row, joined, first, back, spread):
    holders, lead, flat = arrived.shape
    waves = lead // 2
    variables = lift.shape[0] // waves
    rank, channels, _ = joined.shape
    kx2 = height.shape[0]
    kx_count = kx2 // 2
    span = rank * PACK
    wide = GROUP * rank

    def whole(a):
        return pl.BlockSpec(a.shape, lambda g: (0,) * a.ndim)

    return pl.pallas_call(
        functools.partial(mix_kernel, base),
        grid=(groups,),
        in_specs=[
            whole(arrived), whole(height), whole(lift), whole(row_sum), whole(bias_row),
            pl.BlockSpec((rank, channels, wide), lambda g: (0, 0, base + g)),
            whole(first), whole(back), whole(spread),
        ],
        out_specs=pl.BlockSpec((kx2, GROUP * channels), lambda g: (0, g)),
        out_shape=jax.ShapeDtypeStruct((kx2, groups * GROUP * channels), jnp.bfloat16),
        scratch_shapes=[
            pltpu.VMEM((variables * waves, height.shape[1]), jnp.bfloat16),
            pltpu.VMEM((groups, kx2, GROUP * channels), jnp.bfloat16),
            pltpu.VMEM((kx_count // PACK, span, span), jnp.bfloat16),
            pltpu.VMEM((rank * wide, GROUP * back.shape[1]), jnp.bfloat16),
            pltpu.VMEM((GROUP * channels, 8 * wide), jnp.bfloat16),
            pltpu.VMEM((rank, kx_count, 2 * wide), jnp.bfloat16),
            pltpu.VMEM((kx2, rank * wide), jnp.bfloat16),
        ],
        compiler_params=pltpu.CompilerParams(vmem_limit_bytes=48 * 2**20),
        cost_estimate=pl.CostEstimate(
            flops=groups * 7 * 10**9, bytes_accessed=8 * 2**20, transcendentals=0
        ),
        name="mix",
    )(arrived, height, lift, row_sum, bias_row, joined, first, back, spread)


def rows_kernel(table, gathered, *rest):
    cols, turned = rest[-2:]
    row_count, waves, channels = turned.shape
    for p in range(2):
        got = dense(table[p * row_count:(p + 1) * row_count, :], gathered[0])
        for m in range(waves):
            turned[:, m, :] = got[:, m * channels:(m + 1) * channels]
        cols[:, p] = turned[...].astype(jnp.bfloat16)


def rows_back(table, gathered, channels, half, halves, earlier):
    holders, kx2, flat = gathered.shape
    row_count = table.shape[0] // 2
    waves = flat // channels
    shape = (row_count, 2, holders * halves * waves, channels)
    extra = [] if earlier is None else [earlier]
    return pl.pallas_call(
        rows_kernel,
        grid=(holders,),
        in_specs=[
            pl.BlockSpec(table.shape, lambda d: (0, 0)),
            pl.BlockSpec((1, kx2, flat), lambda d: (d, 0, 0)),
        ] + [pl.BlockSpec(memory_space=pl.ANY) for _ in extra],
        input_output_aliases={2: 0} if extra else {},
        cost_estimate=pl.CostEstimate(
            flops=2 * holders * kx2 * kx2 * flat, bytes_accessed=16 * 2**20, transcendentals=0
        ),
        out_specs=pl.BlockSpec((row_count, 2, waves, channels), lambda d: (0, 0, d * halves + half, 0)),
        out_shape=jax.ShapeDtypeStruct(shape, jnp.bfloat16),
        scratch_shapes=[pltpu.VMEM((row_count, waves, channels), jnp.float32)],
        compiler_params=pltpu.CompilerParams(vmem_limit_bytes=48 * 2**20),
        name="rows_back",
    )(table, gathered, *extra)


LANES = 512
HALF = PACK // 2


def gelu(h):
    return h * (0.5 + 0.5 * lax.erf(h * (1.0 / math.sqrt(2.0))))


def finish_kernel(fields, cols, width, skip, bias, closing, out_bias, result, turned, source, active):
    variables, rows, points = fields.shape
    channels = cols.shape[2]
    for x in range(rows):
        turned[x * channels:(x + 1) * channels, :] = cols[x].T
    for h in range(2):
        source[h] = fields[:, h * HALF:(h + 1) * HALF, :].reshape(variables * HALF, points)

    def step(i, carry):
        start = pl.multiple_of(i * LANES, LANES)
        lanes = pl.ds(start, LANES)
        table = width[:, lanes]
        depth = 2 * channels
        for h in range(2):
            near = source[h, :, lanes]
            for x in range(HALF // 2):
                here = slice(x * depth, (x + 1) * depth)
                top = h * HALF * channels + x * depth
                total = dense(turned[top:top + depth, :], table) + dense(skip[here, :], near) + bias[here, :]
                active[here, :] = gelu(total).astype(jnp.bfloat16)
            got = dense(closing[...], active[...]) + out_bias[...]
            result[:, h * HALF:(h + 1) * HALF, lanes] = got.reshape(variables, HALF, LANES).astype(jnp.bfloat16)
        return carry

    lax.fori_loop(0, points // LANES, step, 0)


def finish(fields, cols, width, skip, bias, closing, out_bias):
    variables, row_count, points = fields.shape
    depth, channels = cols.shape[1:]

    def whole(a):
        return pl.BlockSpec(a.shape, lambda i: (0,) * a.ndim)

    return pl.pallas_call(
        finish_kernel,
        grid=(row_count // PACK,),
        in_specs=[
            pl.BlockSpec((variables, PACK, points), lambda i: (0, i, 0)),
            pl.BlockSpec((PACK, depth, channels), lambda i: (i, 0, 0)),
            whole(width), whole(skip), whole(bias), whole(closing), whole(out_bias),
        ],
        out_specs=pl.BlockSpec((variables, PACK, points), lambda i: (0, i, 0)),
        out_shape=jax.ShapeDtypeStruct(fields.shape, jnp.bfloat16),
        scratch_shapes=[
            pltpu.VMEM((PACK * channels, depth), jnp.bfloat16),
            pltpu.VMEM((2, variables * HALF, points), jnp.bfloat16),
            pltpu.VMEM((HALF * channels, LANES), jnp.bfloat16),
        ],
        compiler_params=pltpu.CompilerParams(vmem_limit_bytes=48 * 2**20),
        name="finish",
    )(fields, cols, width, skip, bias, closing, out_bias)


def gather_factors(first_core, input_core, output_core):
    count, rank, _ = first_core.shape
    first_core = first_core.reshape(count // PACK, PACK, rank, rank).transpose(0, 2, 1, 3)
    flat = jnp.concatenate(
        [first_core.reshape(-1), input_core.reshape(-1), output_core.reshape(-1)]
    ).reshape(-1, 128)
    whole = lax.all_gather(flat, "batch", axis=0, tiled=False)
    parts = whole.shape[0]
    size = first_core.size
    whole = whole.reshape(parts, -1)
    first = whole[:, :size].reshape(-1, rank)
    inner = whole[:, size:2 * size].reshape(parts * count, rank, rank)
    outer = whole[:, 2 * size:].reshape(parts * count, 2, rank, rank)
    return first, inner, outer


def fast_shards(
    fields, lift_weight, lift_bias, first_core, second_core, input_core, output_core,
    skip_weight, skip_bias, out_weight, out_bias,
):
    holders = lax.axis_size("mode") * lax.axis_size("cores")
    waves, rank, _ = second_core.shape
    _, variables, row_count, points = fields.shape
    channels = lift_weight.shape[1]
    fields = fields[0]
    me = lax.axis_index("mode") * lax.axis_size("cores") + lax.axis_index("cores")

    cosines, sines = host_pair(np.arange(MY), np.arange(points), points)
    root = math.sqrt(points)
    forward = np.stack([cosines, -sines], 0).reshape(2, holders, waves, points).transpose(1, 0, 2, 3)
    forward = jnp.asarray((forward.reshape(2 * MY, points) / root).astype(np.float32)).astype(jnp.bfloat16)
    weight = np.where(np.arange(MY) == 0, 1.0, 2.0).astype(np.float32)[:, None]
    width = np.concatenate([cosines * weight, -sines * weight], 0) / root
    width = jnp.asarray(width.astype(ml_dtypes.bfloat16))
    order = cyclic_rows(row_count, holders)
    root = math.sqrt(NX)
    cosines, sines = host_pair(np.arange(MX) - MX // 2, order, NX)
    cosines, sines = [t.reshape(MX, holders, row_count) / root for t in (cosines, sines)]
    upper = np.stack([cosines, sines], 2)
    lower = np.stack([-sines, cosines], 2)
    height = np.stack([upper, lower], 0).reshape(2 * MX, -1).astype(ml_dtypes.bfloat16)
    real_part = np.asarray(height, np.float32).reshape(2 * MX, holders, 2, row_count)[:, :, 0]
    row_sum = real_part.sum((1, 2), dtype=np.float64).astype(np.float32)[:, None]
    cos_t, sin_t = [t.transpose(1, 2, 0) for t in (cosines, sines)]
    up = np.concatenate([cos_t, -sin_t], 2)
    low = np.concatenate([sin_t, cos_t], 2)
    back_rows = jnp.asarray(np.concatenate([up, low], 1).astype(ml_dtypes.bfloat16))
    back_rows = lax.dynamic_index_in_dim(back_rows, me, 0, keepdims=False)

    first, inner, outer = gather_factors(first_core, input_core, output_core)
    modes = jnp.einsum(
        "ry,vxy->rvx", forward, fields, preferred_element_type=jnp.float32
    ).astype(jnp.bfloat16)
    modes = modes.reshape(holders, 2 * waves, variables * row_count)
    arrived = lax.all_to_all(modes, ("mode", "cores"), split_axis=0, concat_axis=0, tiled=True)

    same = jnp.eye(waves, dtype=jnp.bfloat16)
    lift = (lift_weight[:, None, None, :] * same[None, :, :, None]).reshape(
        variables * waves, waves * channels
    )
    is_zero = (me * waves + jnp.arange(waves) == 0).astype(jnp.float32)
    bias_value = (math.sqrt(points) * lift_bias).astype(jnp.bfloat16).astype(jnp.float32)
    bias_row = (is_zero[:, None] * bias_value[None, :]).reshape(1, -1)
    joined = jnp.einsum(
        "mbd,cde->bcme", second_core, inner, preferred_element_type=jnp.float32
    ).astype(jnp.bfloat16).reshape(rank, channels, waves * rank)
    back = outer.transpose(3, 2, 1, 0).reshape(rank * rank, -1)
    spread = jnp.asarray(np.repeat(np.eye(rank), PACK, axis=1).astype(ml_dtypes.bfloat16))
    halves = 2
    groups = waves // GROUP // halves
    row_sum = jnp.asarray(row_sum)
    height = jnp.asarray(height)
    mixed = [
        mix(h * groups, groups, arrived, height, lift, row_sum, bias_row, joined, first, back, spread)
        for h in range(halves)
    ]
    gathered = [lax.all_gather(m, ("mode", "cores"), axis=0, tiled=False) for m in mixed]
    cols = None
    for h in range(halves):
        cols = rows_back(back_rows, gathered[h], channels, h, halves, cols)
    cols = cols.reshape(row_count, 2 * MY, channels)

    skip_wide = skip_weight.astype(jnp.float32)
    direct = jnp.dot(lift_weight.astype(jnp.float32), skip_wide, precision="highest")
    total_bias = jnp.dot(lift_bias, skip_wide, precision="highest") + skip_bias
    rows_eye = jnp.eye(HALF, dtype=jnp.float32)
    skip = (rows_eye[:, None, None, :] * direct.T[None, :, :, None]).astype(jnp.bfloat16)
    skip = skip.reshape(HALF * channels, variables * HALF)
    closing = out_weight.T[:, None, None, :] * rows_eye.astype(jnp.bfloat16)[None, :, :, None]
    closing = closing.reshape(variables * HALF, HALF * channels)
    bias = jnp.tile(total_bias, HALF)[:, None]
    last_bias = jnp.repeat(out_bias, HALF)[:, None]
    return finish(fields, cols, width, skip, bias, closing, last_bias)[None]


def solution(mesh):
    placed = (
        P("batch", None, ("mode", "cores"), None),
        P(),
        P(),
        P("batch", None, None),
        P(("mode", "cores"), None, None),
        P("batch", None, None),
        P("batch", None, None, None),
        P(),
        P(),
        P(),
        P(),
    )
    holders = mesh.shape["mode"] * mesh.shape["cores"]
    fits = MX // mesh.shape["batch"] % PACK == 0 and MY // holders % PACK == 0 and NX // holders % 128 == 0
    return jax.shard_map(
        fast_shards if fits else shards,
        mesh=mesh,
        in_specs=placed,
        out_specs=P("batch", None, ("mode", "cores"), None),
        check_vma=False,
    )
```
